32 devices in a mesh: wave: 8 (over y, x, core), atom: 4 (over z).
Axes of the slice: x: 2, y: 2, z: 4, core: 2. Of those that a mesh axis runs over, the one named last changes fastest.
Arguments:
- slab: float32 [4096, 512], P('wave', 'atom'), may hold values from -0.09375 to 0.09375
- orbitals: float32 [4096, 256], P('wave'), may hold values from -6 to 6
- sphere_ops: float32 [3, 8, 64, 64], P(None, 'atom'), may hold values from -0.75 to 0.75
- wave_terms: float32 [3, 4096], P(None, 'wave'), may hold values from -1 to 1
Outputs:
- applied: float32 [3, 4096, 256], P(None, ('wave', 'atom'))
The draws below stay inside these ranges and needn't reach their ends.
All inputs are finite; a program needn't handle non-finite values.
Results may differ from the reference program's by a relative error of at most 0.0001.
Values sent between devices are 32-bit elements; how exact they have to be, the bound alone decides.
A program may use at most 64 MiB of HBM per device.

```python
import jax
import jax.numpy as jnp
from jax import lax

LM = 64
NB = 256
NW = 4096
ATOMS = 8
NS = 512


def shard_levels(own_key, extent, cuts, low, high):
    def one(axis_at, parts):
        steps = jax.random.uniform(jax.random.fold_in(jax.random.fold_in(own_key, 6), axis_at), (parts,), jnp.float32, low / len(cuts), high / len(cuts))
        return jnp.repeat(jnp.exp(steps), extent[axis_at] // parts).reshape((-1,) + (1,) * (len(extent) - axis_at - 1))

    factor_of = one(*cuts[0])
    for cut in cuts[1:]:
        factor_of = factor_of * one(*cut)
    return factor_of


def normal_values(stream_key, extent, deviation, reach, pieces=(), kind=jnp.bfloat16):
    entries = jax.random.normal(stream_key, extent, jnp.float32) * deviation
    if len(pieces) > 0:
        entries = shard_levels(stream_key, extent, pieces, -0.22, 0.18) * entries
    return jnp.clip(entries, min=-reach, max=reach).astype(kind)


def setup_inputs(seed: int = 0) -> dict:
    key_of = jax.random.split(jax.random.key(seed), 5)
    slab = normal_values(key_of[0], (NW, NS), NW ** -0.5, 0.09375, ((0, 8), (1, 4)), jnp.float32)
    orbitals = normal_values(key_of[1], (NW, NB), 1.0, 6.0, ((0, 8),), jnp.float32)
    sphere_ops = normal_values(key_of[2], (3, ATOMS, LM, LM), LM ** -0.5, 0.75, ((1, 4),), jnp.float32)
    wave_terms = jnp.clip(jax.random.uniform(key_of[3], (3, NW), jnp.float32, -1.0, 1.0) * shard_levels(key_of[3], (3, NW), ((1, 8),), -0.4, 0.0), -1.0, 1.0)
    return dict(slab=slab, orbitals=orbitals, sphere_ops=sphere_ops, wave_terms=wave_terms)


def reference(slab, orbitals, sphere_ops, wave_terms):
    coeffs = jnp.dot(slab.T, orbitals, preferred_element_type=jnp.float32, precision=lax.Precision.HIGHEST)
    blocks = coeffs.reshape(ATOMS, LM, NB)
    outs = []
    for direction in range(3):
        inner = jnp.einsum("alm,amb->alb", sphere_ops[direction], blocks, precision=lax.Precision.HIGHEST).reshape(NS, NB)
        sphere_part = jnp.dot(slab, inner, preferred_element_type=jnp.float32, precision=lax.Precision.HIGHEST)
        outs.append(sphere_part + wave_terms[direction][:, None] * orbitals)
    return jnp.stack(outs, 0)
```

```python
import functools

import jax
import jax.numpy as jnp
from jax import lax
from jax.experimental import pallas as pl
from jax.experimental.pallas import tpu as pltpu
from jax.sharding import PartitionSpec as P

MESH = pl.DeviceIdType.MESH


def general_shards(slab, orbitals, sphere_ops, wave_terms):
    partial_value = jnp.dot(
        slab.T, orbitals, preferred_element_type=jnp.float32, precision=lax.Precision.HIGHEST
    )
    coeffs = lax.psum(partial_value, "wave")
    atoms_here = sphere_ops.shape[1]
    width = sphere_ops.shape[2]
    blocks = coeffs.reshape(atoms_here, width, coeffs.shape[1])
    inner = jnp.einsum("dalm,amb->dalb", sphere_ops, blocks, precision=lax.Precision.HIGHEST)
    inner = inner.reshape(inner.shape[0], atoms_here * width, coeffs.shape[1])
    own_rows = orbitals.shape[0] // lax.axis_size("atom")
    first_row = lax.axis_index("atom") * own_rows
    own_orbitals = lax.dynamic_slice_in_dim(orbitals, first_row, own_rows, 0)
    own_factors = lax.dynamic_slice_in_dim(wave_terms, first_row, own_rows, 1)
    local_part = own_factors[:, :, None] * own_orbitals[None]
    terms = jnp.einsum("ws,dsb->dwb", slab, inner, precision=lax.Precision.HIGHEST)
    summed = lax.psum_scatter(terms, "atom", scatter_dimension=1, tiled=True)
    return summed + local_part


def halves(value):
    high = value.astype(jnp.bfloat16)
    low = (value - high.astype(jnp.float32)).astype(jnp.bfloat16)
    return high, low


def product(left, right, dims=((1,), (0,))):
    dot = functools.partial(
        lax.dot_general, dimension_numbers=(dims, ((), ())), preferred_element_type=jnp.float32
    )
    return dot(left[0], right[0]) + (dot(left[0], right[1]) + dot(left[1], right[0]))


def kernel(nw, na, slab_ref, orb_ref, ops_ref, wt_ref, out_ref,
           ops_own, ops_got, ops_all, slab_got, part, sums_got, piece, coeffs, left_side,
           ops_z, slab_z, rs, co_z, ops_p, co_p, ops_f, co_f):
    w = lax.axis_index("wave")
    a = lax.axis_index("atom")
    sister = w + 1 - 2 * lax.rem(w, 2)
    chips = nw // 2
    directions, atoms, width, _ = ops_ref.shape
    rows = slab_ref.shape[0] // na
    functions = slab_ref.shape[1]
    share = functions // nw
    ops_share = directions * width // nw

    def plane(k):
        return lax.rem(w + k, nw)

    def line(k):
        return lax.rem(a + k, na)

    barrier = pltpu.get_barrier_semaphore()
    for k in range(1, nw):
        pl.semaphore_signal(barrier, inc=1, device_id=(plane(k), a), device_id_type=MESH)
    for k in range(1, na):
        pl.semaphore_signal(barrier, inc=1, device_id=(w, line(k)), device_id_type=MESH)

    for d in range(directions):
        for i in range(atoms):
            ops_own[pl.ds(d * width, width), pl.ds(i * width, width)] = ops_ref[d, i]

    pl.semaphore_wait(barrier, nw - 1 + na - 1)

    def send(src, dst, sems, slot, device):
        copy = pltpu.make_async_remote_copy(
            src_ref=src, dst_ref=dst, send_sem=sems.at[0, slot], recv_sem=sems.at[1, slot],
            device_id=device, device_id_type=MESH,
        )
        copy.start()
        return copy

    own_ops_rows = pl.ds(pl.multiple_of(w * ops_share, 8), ops_share)
    ops_line = [
        send(ops_own.at[own_ops_rows], ops_got.at[na - 1 - k], ops_z, k, (w, line(k))) for k in range(1, na)
    ]
    slab_line = [
        send(slab_ref.at[pl.ds(pl.multiple_of(line(k) * rows, 8), rows)], slab_got.at[na - 1 - k],
             slab_z, k, (w, line(k)))
        for k in range(1, na)
    ]

    total = product(halves(slab_ref[...]), halves(orb_ref[...]), ((0,), (0,)))
    part[...] = total.reshape(part.shape)
    pieces = [
        send(part.at[plane(k)], sums_got.at[k - 1], rs, k, (plane(k), a)) for k in range(1, nw)
    ]

    own_rows = pl.ds(pl.multiple_of(a * rows, 128), rows)
    own_orbitals = orb_ref[own_rows, :]
    on_diagonal = lax.broadcasted_iota(jnp.int32, (rows, rows), 0) == lax.broadcasted_iota(
        jnp.int32, (rows, rows), 1)
    for d in range(directions):
        factors = jnp.broadcast_to(wt_ref[pl.ds(d, 1), own_rows], (rows, rows))
        column = jnp.sum(jnp.where(on_diagonal, factors, 0.0), axis=1, keepdims=True)
        out_ref[d] = column * own_orbitals

    mine = part[w]
    for k in range(1, nw):
        pieces[k - 1].wait_recv()
        mine = mine + sums_got[k - 1]
    piece[na - 1] = mine
    co_line = [
        send(piece.at[na - 1], piece.at[na - 1 - k], co_z, k, (w, line(k))) for k in range(1, na)
    ]

    for copy in ops_line:
        copy.wait_recv()
    ops_plane = [
        send(ops_got, ops_all.at[w], ops_p, q, (lax.rem(w + 2 * q, nw), a)) for q in range(1, chips)
    ]
    ops_plane.append(send(ops_got, ops_all.at[w], ops_p, 0, (sister, a)))
    ops_all[w] = ops_got[...]

    for copy in co_line:
        copy.wait_recv()
    co_plane = [
        send(piece, coeffs.at[w], co_p, q, (lax.rem(w + 2 * q, nw), a)) for q in range(1, chips)
    ]
    co_plane.append(send(piece, coeffs.at[w], co_p, 0, (sister, a)))
    coeffs[w] = piece[...]

    def forward(arrived, buffer, sems):
        copies = []
        for q in range(1, chips):
            arrived[q - 1].wait_recv()
            source = lax.rem(w - 2 * q + nw, nw)
            copies.append(send(buffer.at[source], buffer.at[source], sems, q, (sister, a)))
        return copies

    ops_sister = forward(ops_plane, ops_all, ops_f)
    co_sister = forward(co_plane, coeffs, co_f)

    ops_plane[-1].wait_recv()
    for copy in ops_sister:
        copy.wait_recv()
    for copy in slab_line:
        copy.wait_recv()
    lane_atom = lax.broadcasted_iota(jnp.int32, (width, functions), 1) // width
    for s in range(na):
        if s == na - 1:
            stacked = ops_own[...]
            own_slab = slab_ref[own_rows, :]
        else:
            stacked = ops_all[:, s].reshape(directions * width, functions)
            own_slab = slab_got[s]
        slab_halves = halves(own_slab)
        for d in range(directions):
            rows_d = stacked[d * width:(d + 1) * width]
            block = jnp.concatenate(
                [jnp.where(lane_atom == i, rows_d, 0.0) for i in range(atoms)], axis=0)
            left_side[pl.ds(d * rows, rows), pl.ds(s * functions, functions)] = product(
                slab_halves, halves(block))

    co_plane[-1].wait_recv()
    for copy in co_sister:
        copy.wait_recv()
    gathered = jnp.concatenate(
        [coeffs[:, s].reshape(functions, orb_ref.shape[1]) for s in range(na)], axis=0)
    coeff_halves = halves(gathered)
    for d in range(directions):
        out_ref[d] += product(halves(left_side[pl.ds(d * rows, rows), :]), coeff_halves)

    for copy in ops_line + slab_line + pieces + co_line + ops_plane + co_plane + ops_sister + co_sister:
        copy.wait_send()


def kernel_shards(nw, na, slab, orbitals, sphere_ops, wave_terms):
    directions, atoms, width, _ = sphere_ops.shape
    waves, functions = slab.shape
    columns = orbitals.shape[1]
    rows = waves // na
    share = functions // nw
    ops_share = directions * width // nw
    f32 = jnp.float32

    def dma(count):
        return pltpu.SemaphoreType.DMA((2, count))

    vmem = pl.BlockSpec(memory_space=pltpu.VMEM)
    return pl.pallas_call(
        functools.partial(kernel, nw, na),
        out_shape=jax.ShapeDtypeStruct((directions, rows, columns), f32),
        in_specs=[vmem] * 4,
        out_specs=vmem,
        scratch_shapes=[
            pltpu.VMEM((directions * width, functions), f32),
            pltpu.VMEM((na - 1, ops_share, functions), f32),
            pltpu.VMEM((nw, na - 1, ops_share, functions), f32),
            pltpu.VMEM((na - 1, rows, functions), f32),
            pltpu.VMEM((nw, share, columns), f32),
            pltpu.VMEM((nw - 1, share, columns), f32),
            pltpu.VMEM((na, share, columns), f32),
            pltpu.VMEM((nw, na, share, columns), f32),
            pltpu.VMEM((directions * rows, na * functions), f32),
            dma(na), dma(na), dma(nw), dma(na),
            dma(nw // 2), dma(nw // 2), dma(nw // 2), dma(nw // 2),
        ],
        compiler_params=pltpu.CompilerParams(
            collective_id=0, has_side_effects=True, vmem_limit_bytes=32 * 1024 * 1024,
        ),
        cost_estimate=pl.CostEstimate(
            flops=6 * waves * functions * columns * (1 + directions), bytes_accessed=2 * 1024 * 1024,
            transcendentals=0),
    )(slab, orbitals, sphere_ops, wave_terms)


def shards(nw, na, slab, orbitals, sphere_ops, wave_terms):
    directions, atoms, width, _ = sphere_ops.shape
    waves, functions = slab.shape
    fits = (
        nw % 2 == 0 and nw > 2 and na > 1
        and functions % (8 * nw) == 0 and (directions * width) % (8 * nw) == 0
        and atoms * width == functions and functions % 128 == 0
        and waves % (128 * na) == 0 and orbitals.shape[1] % 128 == 0
    )
    if fits:
        return kernel_shards(nw, na, slab, orbitals, sphere_ops, wave_terms)
    return general_shards(slab, orbitals, sphere_ops, wave_terms)


def solution(mesh):
    return jax.shard_map(
        functools.partial(shards, mesh.shape["wave"], mesh.shape["atom"]),
        mesh=mesh,
        in_specs=(P("wave", "atom"), P("wave", None), P(None, "atom", None, None), P(None, "wave")),
        out_specs=P(None, ("wave", "atom"), None),
        check_vma=False,
    )
```

```python
import functools

import jax
import jax.numpy as jnp
from jax import lax
from jax.experimental import pallas as pl
from jax.experimental.pallas import tpu as pltpu
from jax.sharding import PartitionSpec as P

MESH = pl.DeviceIdType.MESH


def general_shards(slab, orbitals, sphere_ops, wave_terms):
    partial_value = jnp.dot(
        slab.T, orbitals, preferred_element_type=jnp.float32, precision=lax.Precision.HIGHEST
    )
    coeffs = lax.psum(partial_value, "wave")
    atoms_here = sphere_ops.shape[1]
    width = sphere_ops.shape[2]
    blocks = coeffs.reshape(atoms_here, width, coeffs.shape[1])
    inner = jnp.einsum("dalm,amb->dalb", sphere_ops, blocks, precision=lax.Precision.HIGHEST)
    inner = inner.reshape(inner.shape[0], atoms_here * width, coeffs.shape[1])
    own_rows = orbitals.shape[0] // lax.axis_size("atom")
    first_row = lax.axis_index("atom") * own_rows
    own_orbitals = lax.dynamic_slice_in_dim(orbitals, first_row, own_rows, 0)
    own_factors = lax.dynamic_slice_in_dim(wave_terms, first_row, own_rows, 1)
    local_part = own_factors[:, :, None] * own_orbitals[None]
    terms = jnp.einsum("ws,dsb->dwb", slab, inner, precision=lax.Precision.HIGHEST)
    summed = lax.psum_scatter(terms, "atom", scatter_dimension=1, tiled=True)
    return summed + local_part


def halves(value):
    high = value.astype(jnp.bfloat16)
    low = (value - high.astype(jnp.float32)).astype(jnp.bfloat16)
    return high, low


def product(left, right, dims=((1,), (0,))):
    dot = functools.partial(
        lax.dot_general, dimension_numbers=(dims, ((), ())), preferred_element_type=jnp.float32
    )
    return dot(left[0], right[0]) + (dot(left[0], right[1]) + dot(left[1], right[0]))


def kernel(nw, na, slab_hbm, orb_hbm, ops_hbm, wt_hbm, out_ref,
           slab_ref, orb_ref, ops_ref, wt_ref, ops_own, ops_got, ops_all, slab_got, part, sums_got, piece,
           coeffs, left_high, left_low, loads, ops_z, slab_z, rs, co_z, ops_p, ops_f, own_p, own_f, co_p, co_f):
    w = lax.axis_index("wave")
    a = lax.axis_index("atom")
    sister = w + 1 - 2 * lax.rem(w, 2)
    chips = nw // 2
    directions, atoms, width, _ = ops_ref.shape
    rows = slab_ref.shape[0] // na
    functions = slab_ref.shape[1]
    ops_share = directions * width // nw
    last = na - 1

    def plane(k):
        return lax.rem(w + k, nw)

    def line(k):
        return lax.rem(a + k, na)

    barrier = pltpu.get_barrier_semaphore()
    for k in range(1, na):
        pl.semaphore_signal(barrier, inc=1, device_id=(w, line(k)), device_id_type=MESH)
    for k in range(1, nw):
        pl.semaphore_signal(barrier, inc=1, device_id=(plane(k), a), device_id_type=MESH)

    local = [
        pltpu.make_async_copy(src, dst, loads.at[n])
        for n, (src, dst) in enumerate(
            ((ops_hbm, ops_ref), (slab_hbm, slab_ref), (orb_hbm, orb_ref), (wt_hbm, wt_ref)))
    ]
    for copy in local:
        copy.start()

    local[0].wait()
    for d in range(directions):
        for i in range(atoms):
            ops_own[pl.ds(d * width, width), pl.ds(i * width, width)] = ops_ref[d, i]

    started = []

    def send(src, dst, sems, slot, device):
        copy = pltpu.make_async_remote_copy(
            src_ref=src, dst_ref=dst, send_sem=sems.at[0, slot], recv_sem=sems.at[1, slot],
            device_id=device, device_id_type=MESH,
        )
        copy.start()
        started.append(copy)
        return copy

    def spread(src, dst, sems):
        copies = [send(src, dst, sems, q, (plane(2 * q), a)) for q in range(1, chips)]
        return copies + [send(src, dst, sems, 0, (sister, a))]

    def forward(arrived, block_of, sems):
        copies = []
        for q in range(1, chips):
            arrived[q - 1].wait_recv()
            block = block_of(lax.rem(w - 2 * q + nw, nw))
            copies.append(send(block, block, sems, q, (sister, a)))
        return copies

    pl.semaphore_wait(barrier, nw - 1 + na - 1)

    own_ops_rows = pl.ds(pl.multiple_of(w * ops_share, 8), ops_share)
    ops_line = [
        send(ops_own.at[own_ops_rows], ops_got.at[last - k], ops_z, k, (w, line(k))) for k in range(1, na)
    ]
    slab_line = [
        send(slab_hbm.at[pl.ds(pl.multiple_of(line(k) * rows, 8), rows)], slab_got.at[last - k],
             slab_z, k, (w, line(k)))
        for k in range(1, na)
    ]

    local[1].wait()
    local[2].wait()
    total = product(halves(slab_ref[...]), halves(orb_ref[...]), ((0,), (0,)))
    part[...] = total.reshape(part.shape)
    pieces = [
        send(part.at[plane(k)], sums_got.at[k - 1], rs, k, (plane(k), a)) for k in range(1, nw)
    ]

    own_rows = pl.ds(pl.multiple_of(a * rows, 128), rows)
    own_orbitals = orb_ref[own_rows, :]
    on_diagonal = lax.broadcasted_iota(jnp.int32, (rows, rows), 0) == lax.broadcasted_iota(
        jnp.int32, (rows, rows), 1)
    local[3].wait()
    for d in range(directions):
        factors = jnp.broadcast_to(wt_ref[pl.ds(d, 1), own_rows], (rows, rows))
        column = jnp.sum(jnp.where(on_diagonal, factors, 0.0), axis=1, keepdims=True)
        out_ref[d] = column * own_orbitals

    lane_atom = lax.broadcasted_iota(jnp.int32, (width, functions), 1) // width

    def apply_blocks(s, own_slab, stacked):
        blocks = [
            jnp.concatenate([
                jnp.where(lane_atom == i, stacked[d * width:(d + 1) * width], 0.0) for i in range(atoms)
            ], axis=0)
            for d in range(directions)
        ]
        high, low = halves(product(halves(own_slab), halves(jnp.concatenate(blocks, axis=1))))
        for d in range(directions):
            at = (pl.ds(d * rows, rows), pl.ds(s * functions, functions))
            left_high[at] = high[:, d * functions:(d + 1) * functions]
            left_low[at] = low[:, d * functions:(d + 1) * functions]

    apply_blocks(last, slab_ref[own_rows, :], ops_own[...])

    for copy in ops_line:
        copy.wait_recv()
    ops_plane = spread(ops_got, ops_all.at[w], ops_p)
    ops_all[w] = ops_got[...]

    mine = part[w]
    for k in range(1, nw):
        pieces[k - 1].wait_recv()
        mine = mine + sums_got[k - 1]
    piece[last] = mine
    co_line = [send(piece.at[last], piece.at[last - k], co_z, k, (w, line(k))) for k in range(1, na)]
    own_plane = spread(piece.at[last], coeffs.at[w, last], own_p)
    ops_sister = forward(ops_plane, lambda source: ops_all.at[source], ops_f)
    for copy in co_line:
        copy.wait_recv()
    others = pl.ds(0, last)
    co_plane = spread(piece.at[others], coeffs.at[w, others], co_p)
    coeffs[w] = piece[...]
    own_sister = forward(own_plane, lambda source: coeffs.at[source, last], own_f)

    ops_plane[-1].wait_recv()
    for copy in ops_sister:
        copy.wait_recv()
    for k in range(1, na):
        s = last - k
        slab_line[k - 1].wait_recv()
        apply_blocks(s, slab_got[s], ops_all[:, s].reshape(directions * width, functions))

    co_sister = forward(co_plane, lambda source: coeffs.at[source, others], co_f)
    for copy in [own_plane[-1], co_plane[-1]] + own_sister + co_sister:
        copy.wait_recv()
    gathered = jnp.concatenate(
        [coeffs[:, s].reshape(functions, orb_ref.shape[1]) for s in range(na)], axis=0)
    coeff_halves = halves(gathered)
    for d in range(directions):
        at = pl.ds(d * rows, rows)
        out_ref[d] += product((left_high[at, :], left_low[at, :]), coeff_halves)

    for copy in started:
        copy.wait_send()


def kernel_shards(nw, na, slab, orbitals, sphere_ops, wave_terms):
    directions, atoms, width, _ = sphere_ops.shape
    waves, functions = slab.shape
    columns = orbitals.shape[1]
    rows = waves // na
    share = functions // nw
    ops_share = directions * width // nw
    f32 = jnp.float32

    def dma(count):
        return pltpu.SemaphoreType.DMA((2, count))

    return pl.pallas_call(
        functools.partial(kernel, nw, na),
        out_shape=jax.ShapeDtypeStruct((directions, rows, columns), f32),
        in_specs=[pl.BlockSpec(memory_space=pltpu.HBM)] * 4,
        out_specs=pl.BlockSpec(memory_space=pltpu.VMEM),
        scratch_shapes=[
            pltpu.VMEM(slab.shape, f32),
            pltpu.VMEM(orbitals.shape, f32),
            pltpu.VMEM(sphere_ops.shape, f32),
            pltpu.VMEM(wave_terms.shape, f32),
            pltpu.VMEM((directions * width, functions), f32),
            pltpu.VMEM((na - 1, ops_share, functions), f32),
            pltpu.VMEM((nw, na - 1, ops_share, functions), f32),
            pltpu.VMEM((na - 1, rows, functions), f32),
            pltpu.VMEM((nw, share, columns), f32),
            pltpu.VMEM((nw - 1, share, columns), f32),
            pltpu.VMEM((na, share, columns), f32),
            pltpu.VMEM((nw, na, share, columns), f32),
            pltpu.VMEM((directions * rows, na * functions), jnp.bfloat16),
            pltpu.VMEM((directions * rows, na * functions), jnp.bfloat16),
            pltpu.SemaphoreType.DMA((4,)),
            dma(na), dma(na), dma(nw), dma(na),
            dma(nw // 2), dma(nw // 2), dma(nw // 2), dma(nw // 2), dma(nw // 2), dma(nw // 2),
        ],
        compiler_params=pltpu.CompilerParams(
            collective_id=0, has_side_effects=True, vmem_limit_bytes=60 * 1024 * 1024,
        ),
        cost_estimate=pl.CostEstimate(
            flops=6 * waves * functions * columns * (1 + directions), bytes_accessed=2 * 1024 * 1024,
            transcendentals=0),
    )(slab, orbitals, sphere_ops, wave_terms)


def shards(nw, na, slab, orbitals, sphere_ops, wave_terms):
    directions, atoms, width, _ = sphere_ops.shape
    waves, functions = slab.shape
    fits = (
        nw % 2 == 0 and nw > 2 and na > 1
        and functions % (8 * nw) == 0 and (directions * width) % (8 * nw) == 0
        and atoms * width == functions and functions % 128 == 0
        and waves % (128 * na) == 0 and orbitals.shape[1] % 128 == 0
    )
    if fits:
        return kernel_shards(nw, na, slab, orbitals, sphere_ops, wave_terms)
    return general_shards(slab, orbitals, sphere_ops, wave_terms)


def solution(mesh):
    return jax.shard_map(
        functools.partial(shards, mesh.shape["wave"], mesh.shape["atom"]),
        mesh=mesh,
        in_specs=(P("wave", "atom"), P("wave", None), P(None, "atom", None, None), P(None, "wave")),
        out_specs=P(None, ("wave", "atom"), None),
        check_vma=False,
    )
```

```python
import functools

import jax
import jax.numpy as jnp
from jax import lax
from jax.experimental import pallas as pl
from jax.experimental.pallas import tpu as pltpu
from jax.sharding import PartitionSpec as P

MESH = pl.DeviceIdType.MESH


def general_shards(slab, orbitals, sphere_ops, wave_terms):
    partial_value = jnp.dot(
        slab.T, orbitals, preferred_element_type=jnp.float32, precision=lax.Precision.HIGHEST
    )
    coeffs = lax.psum(partial_value, "wave")
    atoms_here = sphere_ops.shape[1]
    width = sphere_ops.shape[2]
    blocks = coeffs.reshape(atoms_here, width, coeffs.shape[1])
    inner = jnp.einsum("dalm,amb->dalb", sphere_ops, blocks, precision=lax.Precision.HIGHEST)
    inner = inner.reshape(inner.shape[0], atoms_here * width, coeffs.shape[1])
    own_rows = orbitals.shape[0] // lax.axis_size("atom")
    first_row = lax.axis_index("atom") * own_rows
    own_orbitals = lax.dynamic_slice_in_dim(orbitals, first_row, own_rows, 0)
    own_factors = lax.dynamic_slice_in_dim(wave_terms, first_row, own_rows, 1)
    local_part = own_factors[:, :, None] * own_orbitals[None]
    terms = jnp.einsum("ws,dsb->dwb", slab, inner, precision=lax.Precision.HIGHEST)
    summed = lax.psum_scatter(terms, "atom", scatter_dimension=1, tiled=True)
    return summed + local_part


def halves(value):
    high = value.astype(jnp.bfloat16)
    low = (value - high.astype(jnp.float32)).astype(jnp.bfloat16)
    return high, low


def product(left, right, dims=((1,), (0,))):
    dot = functools.partial(
        lax.dot_general, dimension_numbers=(dims, ((), ())), preferred_element_type=jnp.float32
    )
    return dot(left[0], right[0]) + (dot(left[0], right[1]) + dot(left[1], right[0]))


def kernel(nw, na, slab_hbm, orb_hbm, ops_hbm, wt_hbm, out_ref,
           slab_ref, orb_ref, ops_ref, wt_ref, ops_own, ops_got, ops_all, slab_got, part, sums_got, piece,
           coeffs, left_high, left_low, loads, ops_z, slab_z, rs, co_z, ops_p, ops_f, own_p, own_f, co_p, co_f):
    w = lax.axis_index("wave")
    a = lax.axis_index("atom")
    sister = w + 1 - 2 * lax.rem(w, 2)
    chips = nw // 2
    directions, atoms, width, _ = ops_ref.shape
    rows = slab_ref.shape[0] // na
    functions = slab_ref.shape[1]
    ops_share = directions * width // nw
    last = na - 1

    def plane(k):
        return lax.rem(w + k, nw)

    def line(k):
        return lax.rem(a + k, na)

    barrier = pltpu.get_barrier_semaphore()
    for k in range(1, na):
        pl.semaphore_signal(barrier, inc=1, device_id=(w, line(k)), device_id_type=MESH)
    for k in range(1, nw):
        pl.semaphore_signal(barrier, inc=1, device_id=(plane(k), a), device_id_type=MESH)

    local = [
        pltpu.make_async_copy(src, dst, loads.at[n])
        for n, (src, dst) in enumerate(
            ((ops_hbm, ops_ref), (slab_hbm, slab_ref), (orb_hbm, orb_ref), (wt_hbm, wt_ref)))
    ]
    for copy in local:
        copy.start()

    local[0].wait()
    for d in range(directions):
        for i in range(atoms):
            ops_own[pl.ds(d * width, width), pl.ds(i * width, width)] = ops_ref[d, i]

    started = []

    def send(src, dst, sems, slot, device):
        copy = pltpu.make_async_remote_copy(
            src_ref=src, dst_ref=dst, send_sem=sems.at[0, slot], recv_sem=sems.at[1, slot],
            device_id=device, device_id_type=MESH,
        )
        copy.start()
        started.append(copy)
        return copy

    def spread(src, dst, sems):
        copies = [send(src, dst, sems, q, (plane(2 * q), a)) for q in range(1, chips)]
        return copies + [send(src, dst, sems, 0, (sister, a))]

    def forward(arrived, block_of, sems):
        copies = []
        for q in range(1, chips):
            arrived[q - 1].wait_recv()
            block = block_of(lax.rem(w - 2 * q + nw, nw))
            copies.append(send(block, block, sems, q, (sister, a)))
        return copies

    local[1].wait()
    local[2].wait()
    total = product(halves(slab_ref[...]), halves(orb_ref[...]), ((0,), (0,)))
    part[...] = total.reshape(part.shape)

    own_rows = pl.ds(pl.multiple_of(a * rows, 128), rows)
    own_orbitals = orb_ref[own_rows, :]
    on_diagonal = lax.broadcasted_iota(jnp.int32, (rows, rows), 0) == lax.broadcasted_iota(
        jnp.int32, (rows, rows), 1)
    local[3].wait()
    for d in range(directions):
        factors = jnp.broadcast_to(wt_ref[pl.ds(d, 1), own_rows], (rows, rows))
        column = jnp.sum(jnp.where(on_diagonal, factors, 0.0), axis=1, keepdims=True)
        out_ref[d] = column * own_orbitals

    lane_atom = lax.broadcasted_iota(jnp.int32, (width, functions), 1) // width

    def apply_blocks(s, own_slab, stacked):
        blocks = [
            jnp.concatenate([
                jnp.where(lane_atom == i, stacked[d * width:(d + 1) * width], 0.0) for i in range(atoms)
            ], axis=0)
            for d in range(directions)
        ]
        high, low = halves(product(halves(own_slab), halves(jnp.concatenate(blocks, axis=1))))
        for d in range(directions):
            at = pl.ds(d * rows, rows)
            left_high[s, at] = high[:, d * functions:(d + 1) * functions]
            left_low[s, at] = low[:, d * functions:(d + 1) * functions]

    apply_blocks(last, slab_ref[own_rows, :], ops_own[...])

    pl.semaphore_wait(barrier, nw - 1 + na - 1)

    pieces = [
        send(part.at[plane(k)], sums_got.at[k - 1], rs, k, (plane(k), a)) for k in range(1, nw)
    ]

    own_ops_rows = pl.ds(pl.multiple_of(w * ops_share, 8), ops_share)
    ops_line = [
        send(ops_own.at[own_ops_rows], ops_got.at[last - k], ops_z, k, (w, line(k))) for k in range(1, na)
    ]
    slab_line = [
        send(slab_hbm.at[pl.ds(pl.multiple_of(line(k) * rows, 8), rows)], slab_got.at[last - k],
             slab_z, k, (w, line(k)))
        for k in range(1, na)
    ]


    mine = part[w]
    for k in range(1, nw):
        pieces[k - 1].wait_recv()
        mine = mine + sums_got[k - 1]
    piece[last] = mine
    co_line = [send(piece.at[last], piece.at[last - k], co_z, k, (w, line(k))) for k in range(1, na)]
    own_plane = spread(piece.at[last], coeffs.at[w, last], own_p)

    for copy in ops_line:
        copy.wait_recv()
    ops_plane = spread(ops_got, ops_all.at[w], ops_p)
    ops_all[w] = ops_got[...]
    ops_sister = forward(ops_plane, lambda source: ops_all.at[source], ops_f)
    upper = (2 * a) // na
    steps = [upper * (i + 1) + (1 - upper) * (last - i) for i in range(last)]
    co_plane = []
    for i, k in enumerate(steps):
        s = last - k
        pltpu.make_async_remote_copy(
            src_ref=piece.at[last], dst_ref=piece.at[s], send_sem=co_z.at[0, k], recv_sem=co_z.at[1, k],
            device_id=(w, line(1)), device_id_type=MESH,
        ).wait_recv()
        co_plane.append(spread(piece.at[s], coeffs.at[w, s], co_p.at[i]))
    coeffs[w] = piece[...]
    own_sister = forward(own_plane, lambda source: coeffs.at[source, last], own_f)

    ops_plane[-1].wait_recv()
    for copy in ops_sister:
        copy.wait_recv()
    for k in range(1, na):
        s = last - k
        slab_line[k - 1].wait_recv()
        apply_blocks(s, slab_got[s], ops_all[:, s].reshape(directions * width, functions))

    def add_slot(s, waits):
        for copy in waits:
            copy.wait_recv()
        coeff_halves = halves(coeffs[:, s].reshape(functions, orb_ref.shape[1]))
        for d in range(directions):
            at = pl.ds(d * rows, rows)
            out_ref[d] += product((left_high[s, at], left_low[s, at]), coeff_halves)

    add_slot(last, [own_plane[-1]] + own_sister)
    co_sister = [
        forward(co_plane[i], lambda source, s=last - k: coeffs.at[source, s], co_f.at[i])
        for i, k in enumerate(steps)
    ]
    for i, k in enumerate(steps):
        add_slot(last - k, [co_plane[i][-1]] + co_sister[i])

    for copy in started:
        copy.wait_send()


def kernel_shards(nw, na, slab, orbitals, sphere_ops, wave_terms):
    directions, atoms, width, _ = sphere_ops.shape
    waves, functions = slab.shape
    columns = orbitals.shape[1]
    rows = waves // na
    share = functions // nw
    ops_share = directions * width // nw
    f32 = jnp.float32

    def dma(count):
        return pltpu.SemaphoreType.DMA((2, count))

    return pl.pallas_call(
        functools.partial(kernel, nw, na),
        out_shape=jax.ShapeDtypeStruct((directions, rows, columns), f32),
        in_specs=[pl.BlockSpec(memory_space=pltpu.HBM)] * 4,
        out_specs=pl.BlockSpec(memory_space=pltpu.VMEM),
        scratch_shapes=[
            pltpu.VMEM(slab.shape, f32),
            pltpu.VMEM(orbitals.shape, f32),
            pltpu.VMEM(sphere_ops.shape, f32),
            pltpu.VMEM(wave_terms.shape, f32),
            pltpu.VMEM((directions * width, functions), f32),
            pltpu.VMEM((na - 1, ops_share, functions), f32),
            pltpu.VMEM((nw, na - 1, ops_share, functions), f32),
            pltpu.VMEM((na - 1, rows, functions), f32),
            pltpu.VMEM((nw, share, columns), f32),
            pltpu.VMEM((nw - 1, share, columns), f32),
            pltpu.VMEM((na, share, columns), f32),
            pltpu.VMEM((nw, na, share, columns), f32),
            pltpu.VMEM((na, directions * rows, functions), jnp.bfloat16),
            pltpu.VMEM((na, directions * rows, functions), jnp.bfloat16),
            pltpu.SemaphoreType.DMA((4,)),
            dma(na), dma(na), dma(nw), dma(na),
            dma(nw // 2), dma(nw // 2), dma(nw // 2), dma(nw // 2),
            pltpu.SemaphoreType.DMA((na - 1, 2, nw // 2)), pltpu.SemaphoreType.DMA((na - 1, 2, nw // 2)),
        ],
        compiler_params=pltpu.CompilerParams(
            collective_id=0, has_side_effects=True, vmem_limit_bytes=60 * 1024 * 1024,
        ),
        cost_estimate=pl.CostEstimate(
            flops=6 * waves * functions * columns * (1 + directions), bytes_accessed=2 * 1024 * 1024,
            transcendentals=0),
    )(slab, orbitals, sphere_ops, wave_terms)


def shards(nw, na, slab, orbitals, sphere_ops, wave_terms):
    directions, atoms, width, _ = sphere_ops.shape
    waves, functions = slab.shape
    fits = (
        nw % 2 == 0 and nw > 2 and na > 1
        and functions % (8 * nw) == 0 and (directions * width) % (8 * nw) == 0
        and atoms * width == functions and functions % 128 == 0
        and waves % (128 * na) == 0 and orbitals.shape[1] % 128 == 0
    )
    if fits:
        return kernel_shards(nw, na, slab, orbitals, sphere_ops, wave_terms)
    return general_shards(slab, orbitals, sphere_ops, wave_terms)


def solution(mesh):
    return jax.shard_map(
        functools.partial(shards, mesh.shape["wave"], mesh.shape["atom"]),
        mesh=mesh,
        in_specs=(P("wave", "atom"), P("wave", None), P(None, "atom", None, None), P(None, "wave")),
        out_specs=P(None, ("wave", "atom"), None),
        check_vma=False,
    )
```

```python
import functools

import jax
import jax.numpy as jnp
from jax import lax
from jax.experimental import pallas as pl
from jax.experimental.pallas import tpu as pltpu
from jax.sharding import PartitionSpec as P

MESH = pl.DeviceIdType.MESH


def general_shards(slab, orbitals, sphere_ops, wave_terms):
    partial_value = jnp.dot(
        slab.T, orbitals, preferred_element_type=jnp.float32, precision=lax.Precision.HIGHEST
    )
    coeffs = lax.psum(partial_value, "wave")
    atoms_here = sphere_ops.shape[1]
    width = sphere_ops.shape[2]
    blocks = coeffs.reshape(atoms_here, width, coeffs.shape[1])
    inner = jnp.einsum("dalm,amb->dalb", sphere_ops, blocks, precision=lax.Precision.HIGHEST)
    inner = inner.reshape(inner.shape[0], atoms_here * width, coeffs.shape[1])
    own_rows = orbitals.shape[0] // lax.axis_size("atom")
    first_row = lax.axis_index("atom") * own_rows
    own_orbitals = lax.dynamic_slice_in_dim(orbitals, first_row, own_rows, 0)
    own_factors = lax.dynamic_slice_in_dim(wave_terms, first_row, own_rows, 1)
    local_part = own_factors[:, :, None] * own_orbitals[None]
    terms = jnp.einsum("ws,dsb->dwb", slab, inner, precision=lax.Precision.HIGHEST)
    summed = lax.psum_scatter(terms, "atom", scatter_dimension=1, tiled=True)
    return summed + local_part


def halves(value):
    high = value.astype(jnp.bfloat16)
    low = (value - high.astype(jnp.float32)).astype(jnp.bfloat16)
    return high, low


def product(left, right, dims=((1,), (0,))):
    dot = functools.partial(
        lax.dot_general, dimension_numbers=(dims, ((), ())), preferred_element_type=jnp.float32
    )
    return dot(left[0], right[0]) + (dot(left[0], right[1]) + dot(left[1], right[0]))


def kernel(nw, na, slab_hbm, orb_hbm, ops_hbm, wt_hbm, out_ref,
           slab_ref, orb_ref, ops_ref, wt_ref, ops_own, ops_got, ops_all, slab_got, part, sums_got, piece,
           coeffs, left_high, left_low, loads, ops_z, slab_z, rs, co_z, ops_p, ops_f, own_p, own_f, co_p, co_f):
    w = lax.axis_index("wave")
    a = lax.axis_index("atom")
    sister = w + 1 - 2 * lax.rem(w, 2)
    chips = nw // 2
    directions, atoms, width, _ = ops_ref.shape
    rows = slab_ref.shape[0] // na
    functions = slab_ref.shape[1]
    ops_share = directions * width // nw
    last = na - 1

    def plane(k):
        return lax.rem(w + k, nw)

    def line(k):
        return lax.rem(a + k, na)

    barrier = pltpu.get_barrier_semaphore()
    for k in range(1, na):
        pl.semaphore_signal(barrier, inc=1, device_id=(w, line(k)), device_id_type=MESH)
    for k in range(1, nw):
        pl.semaphore_signal(barrier, inc=1, device_id=(plane(k), a), device_id_type=MESH)

    local = [
        pltpu.make_async_copy(src, dst, loads.at[n])
        for n, (src, dst) in enumerate(
            ((ops_hbm, ops_ref), (slab_hbm, slab_ref), (orb_hbm, orb_ref), (wt_hbm, wt_ref)))
    ]
    for copy in local:
        copy.start()

    local[0].wait()
    for d in range(directions):
        for i in range(atoms):
            ops_own[pl.ds(d * width, width), pl.ds(i * width, width)] = ops_ref[d, i]

    started = []

    def send(src, dst, sems, slot, device):
        copy = pltpu.make_async_remote_copy(
            src_ref=src, dst_ref=dst, send_sem=sems.at[0, slot], recv_sem=sems.at[1, slot],
            device_id=device, device_id_type=MESH,
        )
        copy.start()
        started.append(copy)
        return copy

    def spread(src, dst, sems):
        copies = [send(src, dst, sems, q, (plane(2 * q), a)) for q in range(1, chips)]
        return copies + [send(src, dst, sems, 0, (sister, a))]

    def forward(arrived, block_of, sems):
        copies = []
        for q in range(1, chips):
            arrived[q - 1].wait_recv()
            block = block_of(lax.rem(w - 2 * q + nw, nw))
            copies.append(send(block, block, sems, q, (sister, a)))
        return copies

    local[1].wait()
    local[2].wait()
    total = product(halves(slab_ref[...]), halves(orb_ref[...]), ((0,), (0,)))
    part[...] = total.reshape(part.shape)

    own_rows = pl.ds(pl.multiple_of(a * rows, 128), rows)
    own_orbitals = orb_ref[own_rows, :]
    on_diagonal = lax.broadcasted_iota(jnp.int32, (rows, rows), 0) == lax.broadcasted_iota(
        jnp.int32, (rows, rows), 1)
    local[3].wait()
    for d in range(directions):
        factors = jnp.broadcast_to(wt_ref[pl.ds(d, 1), own_rows], (rows, rows))
        column = jnp.sum(jnp.where(on_diagonal, factors, 0.0), axis=1, keepdims=True)
        out_ref[d] = column * own_orbitals

    lane_atom = lax.broadcasted_iota(jnp.int32, (width, functions), 1) // width

    def apply_blocks(s, own_slab, stacked):
        blocks = [
            jnp.concatenate([
                jnp.where(lane_atom == i, stacked[d * width:(d + 1) * width], 0.0) for i in range(atoms)
            ], axis=0)
            for d in range(directions)
        ]
        high, low = halves(product(halves(own_slab), halves(jnp.concatenate(blocks, axis=1))))
        for d in range(directions):
            at = pl.ds(d * rows, rows)
            left_high[s, at] = high[:, d * functions:(d + 1) * functions]
            left_low[s, at] = low[:, d * functions:(d + 1) * functions]

    apply_blocks(last, slab_ref[own_rows, :], ops_own[...])

    pl.semaphore_wait(barrier, nw - 1 + na - 1)

    pieces = [
        send(part.at[plane(k)], sums_got.at[k - 1], rs, k, (plane(k), a)) for k in range(1, nw)
    ]

    own_ops_rows = pl.ds(pl.multiple_of(w * ops_share, 8), ops_share)
    ops_line = [
        send(ops_own.at[own_ops_rows], ops_got.at[last - k], ops_z, k, (w, line(k))) for k in range(1, na)
    ]
    slab_line = [
        send(slab_hbm.at[pl.ds(pl.multiple_of(line(k) * rows, 8), rows)], slab_got.at[last - k],
             slab_z, k, (w, line(k)))
        for k in range(1, na)
    ]

    mine = part[w]
    for k in range(1, nw):
        pieces[k - 1].wait_recv()
        mine = mine + sums_got[k - 1]
    piece[last] = mine
    co_line = [send(piece.at[last], piece.at[last - k], co_z, k, (w, line(k))) for k in range(1, na)]
    own_plane = spread(piece.at[last], coeffs.at[w, last], own_p)

    for copy in ops_line:
        copy.wait_recv()
    ops_plane = spread(ops_got, ops_all.at[w], ops_p)
    ops_all[w] = ops_got[...]

    upper = (2 * a) // na
    steps = [upper * (i + 1) + (1 - upper) * (last - i) for i in range(last)]
    co_plane = []
    for i, k in enumerate(steps):
        s = last - k
        pltpu.make_async_remote_copy(
            src_ref=piece.at[last], dst_ref=piece.at[s], send_sem=co_z.at[0, k], recv_sem=co_z.at[1, k],
            device_id=(w, line(1)), device_id_type=MESH,
        ).wait_recv()
        co_plane.append(spread(piece.at[s], coeffs.at[w, s], co_p.at[i]))
    coeffs[w] = piece[...]
    ops_sister = forward(ops_plane, lambda source: ops_all.at[source], ops_f)
    own_sister = forward(own_plane, lambda source: coeffs.at[source, last], own_f)

    ops_plane[-1].wait_recv()
    for copy in ops_sister:
        copy.wait_recv()
    for k in range(1, na):
        s = last - k
        slab_line[k - 1].wait_recv()
        apply_blocks(s, slab_got[s], ops_all[:, s].reshape(directions * width, functions))

    def add_slot(s, waits):
        for copy in waits:
            copy.wait_recv()
        coeff_halves = halves(coeffs[:, s].reshape(functions, orb_ref.shape[1]))
        for d in range(directions):
            at = pl.ds(d * rows, rows)
            out_ref[d] += product((left_high[s, at], left_low[s, at]), coeff_halves)

    add_slot(last, [own_plane[-1]] + own_sister)
    co_sister = [
        forward(co_plane[i], lambda source, s=last - k: coeffs.at[source, s], co_f.at[i])
        for i, k in enumerate(steps)
    ]
    for i, k in enumerate(steps):
        add_slot(last - k, [co_plane[i][-1]] + co_sister[i])

    for copy in started:
        copy.wait_send()


def kernel_shards(nw, na, slab, orbitals, sphere_ops, wave_terms):
    directions, atoms, width, _ = sphere_ops.shape
    waves, functions = slab.shape
    columns = orbitals.shape[1]
    rows = waves // na
    share = functions // nw
    ops_share = directions * width // nw
    f32 = jnp.float32

    def dma(count):
        return pltpu.SemaphoreType.DMA((2, count))

    return pl.pallas_call(
        functools.partial(kernel, nw, na),
        out_shape=jax.ShapeDtypeStruct((directions, rows, columns), f32),
        in_specs=[pl.BlockSpec(memory_space=pltpu.HBM)] * 4,
        out_specs=pl.BlockSpec(memory_space=pltpu.VMEM),
        scratch_shapes=[
            pltpu.VMEM(slab.shape, f32),
            pltpu.VMEM(orbitals.shape, f32),
            pltpu.VMEM(sphere_ops.shape, f32),
            pltpu.VMEM(wave_terms.shape, f32),
            pltpu.VMEM((directions * width, functions), f32),
            pltpu.VMEM((na - 1, ops_share, functions), f32),
            pltpu.VMEM((nw, na - 1, ops_share, functions), f32),
            pltpu.VMEM((na - 1, rows, functions), f32),
            pltpu.VMEM((nw, share, columns), f32),
            pltpu.VMEM((nw - 1, share, columns), f32),
            pltpu.VMEM((na, share, columns), f32),
            pltpu.VMEM((nw, na, share, columns), f32),
            pltpu.VMEM((na, directions * rows, functions), jnp.bfloat16),
            pltpu.VMEM((na, directions * rows, functions), jnp.bfloat16),
            pltpu.SemaphoreType.DMA((4,)),
            dma(na), dma(na), dma(nw), dma(na),
            dma(nw // 2), dma(nw // 2), dma(nw // 2), dma(nw // 2),
            pltpu.SemaphoreType.DMA((na - 1, 2, nw // 2)), pltpu.SemaphoreType.DMA((na - 1, 2, nw // 2)),
        ],
        compiler_params=pltpu.CompilerParams(
            collective_id=0, has_side_effects=True, vmem_limit_bytes=60 * 1024 * 1024,
        ),
        cost_estimate=pl.CostEstimate(
            flops=6 * waves * functions * columns * (1 + directions), bytes_accessed=2 * 1024 * 1024,
            transcendentals=0),
    )(slab, orbitals, sphere_ops, wave_terms)


def shards(nw, na, slab, orbitals, sphere_ops, wave_terms):
    directions, atoms, width, _ = sphere_ops.shape
    waves, functions = slab.shape
    fits = (
        nw % 2 == 0 and nw > 2 and na > 1
        and functions % (8 * nw) == 0 and (directions * width) % (8 * nw) == 0
        and atoms * width == functions and functions % 128 == 0
        and waves % (128 * na) == 0 and orbitals.shape[1] % 128 == 0
    )
    if fits:
        return kernel_shards(nw, na, slab, orbitals, sphere_ops, wave_terms)
    return general_shards(slab, orbitals, sphere_ops, wave_terms)


def solution(mesh):
    return jax.shard_map(
        functools.partial(shards, mesh.shape["wave"], mesh.shape["atom"]),
        mesh=mesh,
        in_specs=(P("wave", "atom"), P("wave", None), P(None, "atom", None, None), P(None, "wave")),
        out_specs=P(None, ("wave", "atom"), None),
        check_vma=False,
    )
```

```python
import functools

import jax
import jax.numpy as jnp
from jax import lax
from jax.experimental import pallas as pl
from jax.experimental.pallas import tpu as pltpu
from jax.sharding import PartitionSpec as P

MESH = pl.DeviceIdType.MESH


def general_shards(slab, orbitals, sphere_ops, wave_terms):
    partial_value = jnp.dot(
        slab.T, orbitals, preferred_element_type=jnp.float32, precision=lax.Precision.HIGHEST
    )
    coeffs = lax.psum(partial_value, "wave")
    atoms_here = sphere_ops.shape[1]
    width = sphere_ops.shape[2]
    blocks = coeffs.reshape(atoms_here, width, coeffs.shape[1])
    inner = jnp.einsum("dalm,amb->dalb", sphere_ops, blocks, precision=lax.Precision.HIGHEST)
    inner = inner.reshape(inner.shape[0], atoms_here * width, coeffs.shape[1])
    own_rows = orbitals.shape[0] // lax.axis_size("atom")
    first_row = lax.axis_index("atom") * own_rows
    own_orbitals = lax.dynamic_slice_in_dim(orbitals, first_row, own_rows, 0)
    own_factors = lax.dynamic_slice_in_dim(wave_terms, first_row, own_rows, 1)
    local_part = own_factors[:, :, None] * own_orbitals[None]
    terms = jnp.einsum("ws,dsb->dwb", slab, inner, precision=lax.Precision.HIGHEST)
    summed = lax.psum_scatter(terms, "atom", scatter_dimension=1, tiled=True)
    return summed + local_part


def halves(value):
    high = value.astype(jnp.bfloat16)
    low = (value - high.astype(jnp.float32)).astype(jnp.bfloat16)
    return high, low


def product(left, right, dims=((1,), (0,))):
    dot = functools.partial(
        lax.dot_general, dimension_numbers=(dims, ((), ())), preferred_element_type=jnp.float32
    )
    return dot(left[0], right[0]) + (dot(left[0], right[1]) + dot(left[1], right[0]))


def kernel(nw, na, slab_hbm, orb_hbm, ops_hbm, wt_hbm, out_ref,
           slab_ref, orb_ref, ops_ref, wt_ref, ops_own, ops_got, ops_all, slab_got, part, sums_got, piece,
           coeffs, left_high, left_low, loads, ops_z, slab_z, rs, co_z, ops_p, ops_f, own_p, own_f, co_p, co_f):
    w = lax.axis_index("wave")
    a = lax.axis_index("atom")
    sister = w + 1 - 2 * lax.rem(w, 2)
    chips = nw // 2
    directions, atoms, width, _ = ops_ref.shape
    rows = slab_ref.shape[0] // na
    functions = slab_ref.shape[1]
    ops_share = directions * width // nw
    last = na - 1

    def plane(k):
        return lax.rem(w + k, nw)

    def line(k):
        return lax.rem(a + k, na)

    barrier = pltpu.get_barrier_semaphore()
    for k in range(1, na):
        pl.semaphore_signal(barrier, inc=1, device_id=(w, line(k)), device_id_type=MESH)
    for k in range(1, nw):
        pl.semaphore_signal(barrier, inc=1, device_id=(plane(k), a), device_id_type=MESH)

    local = [
        pltpu.make_async_copy(src, dst, loads.at[n])
        for n, (src, dst) in enumerate(
            ((ops_hbm, ops_ref), (slab_hbm, slab_ref), (orb_hbm, orb_ref), (wt_hbm, wt_ref)))
    ]
    for copy in local:
        copy.start()

    local[0].wait()
    for d in range(directions):
        for i in range(atoms):
            ops_own[pl.ds(d * width, width), pl.ds(i * width, width)] = ops_ref[d, i]

    started = []

    def send(src, dst, sems, slot, device):
        copy = pltpu.make_async_remote_copy(
            src_ref=src, dst_ref=dst, send_sem=sems.at[0, slot], recv_sem=sems.at[1, slot],
            device_id=device, device_id_type=MESH,
        )
        copy.start()
        started.append(copy)
        return copy

    def spread(src, dst, sems):
        copies = [send(src, dst, sems, q, (plane(2 * q), a)) for q in range(1, chips)]
        return copies + [send(src, dst, sems, 0, (sister, a))]

    def forward(arrived, block_of, sems):
        copies = []
        for q in range(1, chips):
            arrived[q - 1].wait_recv()
            block = block_of(lax.rem(w - 2 * q + nw, nw))
            copies.append(send(block, block, sems, q, (sister, a)))
        return copies

    local[1].wait()
    local[2].wait()
    total = product(halves(slab_ref[...]), halves(orb_ref[...]), ((0,), (0,)))
    part[...] = total.reshape(part.shape)

    own_rows = pl.ds(pl.multiple_of(a * rows, 128), rows)
    own_orbitals = orb_ref[own_rows, :]
    on_diagonal = lax.broadcasted_iota(jnp.int32, (rows, rows), 0) == lax.broadcasted_iota(
        jnp.int32, (rows, rows), 1)
    local[3].wait()
    for d in range(directions):
        factors = jnp.broadcast_to(wt_ref[pl.ds(d, 1), own_rows], (rows, rows))
        column = jnp.sum(jnp.where(on_diagonal, factors, 0.0), axis=1, keepdims=True)
        out_ref[d] = column * own_orbitals

    lane_atom = lax.broadcasted_iota(jnp.int32, (width, functions), 1) // width

    def apply_blocks(s, own_slab, stacked):
        blocks = [
            jnp.concatenate([
                jnp.where(lane_atom == i, stacked[d * width:(d + 1) * width], 0.0) for i in range(atoms)
            ], axis=0)
            for d in range(directions)
        ]
        high, low = halves(product(halves(own_slab), halves(jnp.concatenate(blocks, axis=1))))
        for d in range(directions):
            at = pl.ds(d * rows, rows)
            left_high[s, at] = high[:, d * functions:(d + 1) * functions]
            left_low[s, at] = low[:, d * functions:(d + 1) * functions]

    apply_blocks(last, slab_ref[own_rows, :], ops_own[...])

    pl.semaphore_wait(barrier, nw - 1 + na - 1)

    pieces = [
        send(part.at[plane(k)], sums_got.at[k - 1], rs, k, (plane(k), a)) for k in range(1, nw)
    ]

    own_ops_rows = pl.ds(pl.multiple_of(w * ops_share, 8), ops_share)
    ops_line = [
        send(ops_own.at[own_ops_rows], ops_got.at[last - k], ops_z, k, (w, line(k))) for k in range(1, na)
    ]
    half = rows // 2

    def send_slab(h):
        return [
            send(slab_hbm.at[pl.ds(pl.multiple_of(line(k) * rows + h * half, 8), half)],
                 slab_got.at[last - k, pl.ds(h * half, half)], slab_z, h * na + k, (w, line(k)))
            for k in range(1, na)
        ]

    slab_line = send_slab(0)

    mine = part[w]
    for k in range(1, nw):
        pieces[k - 1].wait_recv()
        mine = mine + sums_got[k - 1]
    piece[last] = mine
    co_line = [send(piece.at[last], piece.at[last - k], co_z, k, (w, line(k))) for k in range(1, na)]
    own_plane = spread(piece.at[last], coeffs.at[w, last], own_p)
    slab_line += send_slab(1)

    for copy in ops_line:
        copy.wait_recv()
    ops_plane = spread(ops_got, ops_all.at[w], ops_p)
    ops_all[w] = ops_got[...]

    upper = (2 * a) // na
    steps = [upper * (i + 1) + (1 - upper) * (last - i) for i in range(last)]
    co_plane = []
    for i, k in enumerate(steps):
        s = last - k
        pltpu.make_async_remote_copy(
            src_ref=piece.at[last], dst_ref=piece.at[s], send_sem=co_z.at[0, k], recv_sem=co_z.at[1, k],
            device_id=(w, line(1)), device_id_type=MESH,
        ).wait_recv()
        co_plane.append(spread(piece.at[s], coeffs.at[w, s], co_p.at[i]))
    coeffs[w] = piece[...]
    ops_sister = forward(ops_plane, lambda source: ops_all.at[source], ops_f)
    own_sister = forward(own_plane, lambda source: coeffs.at[source, last], own_f)

    ops_plane[-1].wait_recv()
    for copy in ops_sister:
        copy.wait_recv()
    for k in range(1, na):
        s = last - k
        slab_line[k - 1].wait_recv()
        slab_line[last + k - 1].wait_recv()
        apply_blocks(s, slab_got[s], ops_all[:, s].reshape(directions * width, functions))

    def add_slot(s, waits):
        for copy in waits:
            copy.wait_recv()
        coeff_halves = halves(coeffs[:, s].reshape(functions, orb_ref.shape[1]))
        for d in range(directions):
            at = pl.ds(d * rows, rows)
            out_ref[d] += product((left_high[s, at], left_low[s, at]), coeff_halves)

    add_slot(last, [own_plane[-1]] + own_sister)
    co_sister = [
        forward(co_plane[i], lambda source, s=last - k: coeffs.at[source, s], co_f.at[i])
        for i, k in enumerate(steps)
    ]
    for i, k in enumerate(steps):
        add_slot(last - k, [co_plane[i][-1]] + co_sister[i])

    for copy in started:
        copy.wait_send()


def kernel_shards(nw, na, slab, orbitals, sphere_ops, wave_terms):
    directions, atoms, width, _ = sphere_ops.shape
    waves, functions = slab.shape
    columns = orbitals.shape[1]
    rows = waves // na
    share = functions // nw
    ops_share = directions * width // nw
    f32 = jnp.float32

    def dma(count):
        return pltpu.SemaphoreType.DMA((2, count))

    return pl.pallas_call(
        functools.partial(kernel, nw, na),
        out_shape=jax.ShapeDtypeStruct((directions, rows, columns), f32),
        in_specs=[pl.BlockSpec(memory_space=pltpu.HBM)] * 4,
        out_specs=pl.BlockSpec(memory_space=pltpu.VMEM),
        scratch_shapes=[
            pltpu.VMEM(slab.shape, f32),
            pltpu.VMEM(orbitals.shape, f32),
            pltpu.VMEM(sphere_ops.shape, f32),
            pltpu.VMEM(wave_terms.shape, f32),
            pltpu.VMEM((directions * width, functions), f32),
            pltpu.VMEM((na - 1, ops_share, functions), f32),
            pltpu.VMEM((nw, na - 1, ops_share, functions), f32),
            pltpu.VMEM((na - 1, rows, functions), f32),
            pltpu.VMEM((nw, share, columns), f32),
            pltpu.VMEM((nw - 1, share, columns), f32),
            pltpu.VMEM((na, share, columns), f32),
            pltpu.VMEM((nw, na, share, columns), f32),
            pltpu.VMEM((na, directions * rows, functions), jnp.bfloat16),
            pltpu.VMEM((na, directions * rows, functions), jnp.bfloat16),
            pltpu.SemaphoreType.DMA((4,)),
            dma(na), dma(2 * na), dma(nw), dma(na),
            dma(nw // 2), dma(nw // 2), dma(nw // 2), dma(nw // 2),
            pltpu.SemaphoreType.DMA((na - 1, 2, nw // 2)), pltpu.SemaphoreType.DMA((na - 1, 2, nw // 2)),
        ],
        compiler_params=pltpu.CompilerParams(
            collective_id=0, has_side_effects=True, vmem_limit_bytes=60 * 1024 * 1024,
        ),
        cost_estimate=pl.CostEstimate(
            flops=6 * waves * functions * columns * (1 + directions), bytes_accessed=2 * 1024 * 1024,
            transcendentals=0),
    )(slab, orbitals, sphere_ops, wave_terms)


def shards(nw, na, slab, orbitals, sphere_ops, wave_terms):
    directions, atoms, width, _ = sphere_ops.shape
    waves, functions = slab.shape
    fits = (
        nw % 2 == 0 and nw > 2 and na > 1
        and functions % (8 * nw) == 0 and (directions * width) % (8 * nw) == 0
        and atoms * width == functions and functions % 128 == 0
        and waves % (128 * na) == 0 and orbitals.shape[1] % 128 == 0
    )
    if fits:
        return kernel_shards(nw, na, slab, orbitals, sphere_ops, wave_terms)
    return general_shards(slab, orbitals, sphere_ops, wave_terms)


def solution(mesh):
    return jax.shard_map(
        functools.partial(shards, mesh.shape["wave"], mesh.shape["atom"]),
        mesh=mesh,
        in_specs=(P("wave", "atom"), P("wave", None), P(None, "atom", None, None), P(None, "wave")),
        out_specs=P(None, ("wave", "atom"), None),
        check_vma=False,
    )
```
